32 devices in a mesh: parts: 2 (over x), seq: 16 (over z, y, core).
Axes of the slice: x: 2, y: 2, z: 4, core: 2. Of those that a mesh axis runs over, the one named last changes fastest.
Arguments:
- tokens: bfloat16 [262144, 512], P(('parts', 'seq')), parts along dimension 0, may hold values from -6 to 6
- cotangent: bfloat16 [262144, 512], P(('parts', 'seq')), parts along dimension 0, may hold values from -0.75 to 0.75
- first_factor: bfloat16 [512, 256, 256], P('seq'), may hold values from -0.375 to 0.375
- second_factor: bfloat16 [256, 512, 512], P('seq'), may hold values from -0.25 to 0.25
- gate_weight: bfloat16 [512, 512], replicated, may hold values from -0.25 to 0.25
Outputs:
- token_grad: bfloat16 [262144, 512], P(('parts', 'seq')), parts along dimension 0
- first_grad: bfloat16 [1024, 256, 256], P(('parts', 'seq')), parts along dimension 0
- second_grad: bfloat16 [512, 512, 512], P(('parts', 'seq')), parts along dimension 0
- gate_grad: bfloat16 [1024, 512], P('parts'), parts along dimension 0
The draws below stay inside these ranges and needn't reach their ends.
There are 2 independent parts, one for each index of `parts`. The reference program is written for one: setup_inputs(seed, part) draws one part's arguments, and reference() takes and returns one part's arrays. A program takes and returns all parts, laid end to end along the dimension named above; an argument that names none is the same for every part. Nothing has to cross between parts.
All inputs are finite; a program needn't handle non-finite values.
Results may differ from the reference program's by a relative error of at most 0.0061.
Values may be sent and summed in bfloat16 or wider, within the bound.
A program may use at most 256 MiB of HBM per device.

```python
import jax
import jax.numpy as jnp
from jax import lax

OUTER = 512
INNER = 256
D = 512
TOKENS = 131072


def levels(rng, extent, pieces, least, largest):
    loudness, own = 1.0, jax.random.fold_in(rng, 6)
    for dim, blocks in pieces:
        steps = jnp.exp(jax.random.uniform(jax.random.fold_in(own, dim), (blocks,), jnp.float32, least / len(pieces), largest / len(pieces)))
        loudness = loudness * jnp.repeat(steps, extent[dim] // blocks).reshape([-1 if axis == dim else 1 for axis in range(len(extent))])
    return loudness


def noise(rng, shape, spread, limit, pieces=(), dtype=jnp.bfloat16):
    gain = levels(rng, shape, pieces, -0.22, 0.18) if pieces else 1.0
    drawn = jax.random.normal(rng, shape, jnp.float32) * spread * gain
    return jnp.minimum(jnp.maximum(drawn, -limit), limit).astype(dtype)


def setup_inputs(seed: int = 0, part: int = 0) -> dict:
    keys = jax.random.split(jax.random.key(seed), 6)
    own_keys = jax.random.split(jax.random.fold_in(keys[5], part), 6)
    return {
        "tokens": noise(own_keys[0], (TOKENS, D), 1.0, 6.0, ((0, 16),)),
        "cotangent": noise(own_keys[1], (TOKENS, D), 0.125, 0.75, ((0, 16),)),
        "first_factor": noise(keys[2], (OUTER, INNER, INNER), INNER ** -0.5, 0.375, ((0, 16),)),
        "second_factor": noise(keys[3], (INNER, OUTER, OUTER), OUTER ** -0.5, 0.25, ((0, 16),)),
        "gate_weight": noise(keys[4], (D, D), D ** -0.5, 0.25),
    }


def reference(tokens, cotangent, first_factor, second_factor, gate_weight):
    width = tokens.shape[1]
    gate = jax.nn.sigmoid(jnp.dot(tokens, gate_weight, preferred_element_type=jnp.float32))
    tok_f = tokens.astype(jnp.float32)
    mixed = (tok_f * gate).astype(jnp.bfloat16)
    mixed3 = mixed.reshape(OUTER, INNER, width)
    middle = jnp.einsum('abk,akc->abc', first_factor.astype(jnp.float32), mixed3.astype(jnp.float32)).astype(jnp.bfloat16)
    back = cotangent.reshape(INNER, OUTER, width)
    middle_back = jnp.einsum('bak,bac->kbc', second_factor.astype(jnp.float32), back.astype(jnp.float32)).astype(jnp.bfloat16)
    second_grad = jnp.einsum('bac,kbc->bak', back.astype(jnp.float32), middle.astype(jnp.float32)).astype(jnp.bfloat16)
    mixed_back = jnp.einsum('abk,abc->akc', first_factor.astype(jnp.float32), middle_back.astype(jnp.float32))
    first_grad = jnp.einsum('abc,akc->abk', middle_back.astype(jnp.float32), mixed3.astype(jnp.float32)).astype(jnp.bfloat16)
    mixed_back = mixed_back.reshape(OUTER * INNER, width)
    slope = (mixed_back * tok_f * gate * (1.0 - gate)).astype(jnp.bfloat16)
    token_grad = mixed_back * gate + lax.dot_general(slope, gate_weight, (((1,), (1,)), ((), ())), preferred_element_type=jnp.float32)
    gate_grad = lax.dot_general(tokens, slope, (((0,), (0,)), ((), ())), preferred_element_type=jnp.float32)
    return token_grad.astype(jnp.bfloat16), first_grad, second_grad, gate_grad.astype(jnp.bfloat16)
```

```python
import functools

import jax
import jax.numpy as jnp
from jax import lax
from jax.experimental import pallas as pl
from jax.experimental.pallas import tpu as pltpu
from jax.sharding import PartitionSpec as P

MESH = pl.DeviceIdType.MESH
F32 = jnp.float32
BF16 = jnp.bfloat16
LANES = 128


def dot(x, y, x_dim, y_dim):
    return lax.dot_general(
        x, y, (((x_dim,), (y_dim,)), ((), ())), preferred_element_type=F32
    )


def send_order(n):
    quarters = [list(range(q * n // 4, (q + 1) * n // 4)) for q in (2, 1, 3, 0)]
    order = [s for group in zip(*quarters) for s in group]
    return [s for s in order if s != 0]


def exchange_kernel(
    n, outer, inner, group,
    tok_ref, cot_ref, ff_ref, sf_ref, w_ref,
    tg_ref, fg_ref, gl_ref, mid_recv,
    mb_send, mb_recv, mb_here, mid_group, mid_send,
    mb_out, mb_in, mb_own, mid_out, mid_in, mid_own,
):
    part, me = lax.axis_index("parts"), lax.axis_index("seq")
    step = pl.program_id(0)
    width = tok_ref.shape[2]
    inner_size = tok_ref.shape[1]
    batch = min(4, inner)
    second, third = inner, inner + outer
    last = inner + 2 * outer - 1
    order = send_order(n)

    def all_bytes(send, recv, out_sem, in_sem):
        return pltpu.make_async_remote_copy(
            src_ref=send.at[pl.ds(0, n - 1)], dst_ref=recv.at[pl.ds(0, n - 1)],
            send_sem=out_sem, recv_sem=in_sem,
            device_id=(part, lax.rem(me + 1, n)), device_id_type=MESH,
        )

    mb_all = all_bytes(mb_send, mb_recv, mb_out, mb_in)
    mid_all = all_bytes(mid_send, mid_recv, mid_out, mid_in)
    mb_local = pltpu.make_async_copy(mb_send.at[me], mb_recv.at[me], mb_own)
    mid_local = pltpu.make_async_copy(mid_send.at[me], mid_recv.at[me], mid_own)

    @pl.when(step == 0)
    def _():
        barrier = pltpu.get_barrier_semaphore()
        for s in range(1, n):
            pl.semaphore_signal(
                barrier, inc=1, device_id=(part, lax.rem(me + s, n)), device_id_type=MESH
            )
        pl.semaphore_wait(barrier, n - 1)

    @pl.when(step < second)
    def _():
        made = dot(sf_ref[0], cot_ref[0], 0, 0)
        mb_send[:, step] = made.reshape(n, outer, width).astype(BF16)

        @pl.when(lax.rem(step, batch) == batch - 1)
        def _():
            rows = pl.ds(step - (batch - 1), batch)
            for s in order:
                to = lax.rem(me + s, n)
                pltpu.make_async_remote_copy(
                    src_ref=mb_send.at[to, rows], dst_ref=mb_recv.at[me, rows],
                    send_sem=mb_out, recv_sem=mb_in,
                    device_id=(part, to), device_id_type=MESH,
                ).start()

    @pl.when(step == second)
    def _():
        mb_local.start()

    def gated():
        tok = tok_ref[0]
        tok_f = tok.astype(F32)
        gate = jax.nn.sigmoid(dot(tok, w_ref[...], 1, 0))
        return tok, tok_f, gate, (tok_f * gate).astype(BF16)

    tall = 16 // inner if inner < 16 else 1
    chunk = tall * inner

    @pl.when((step >= second) & (step < third))
    def _():
        at = step - second
        _, _, _, mixed = gated()
        slot = lax.rem(at, group)
        mid_group[slot] = dot(ff_ref[0], mixed, 1, 0).astype(BF16)

        @pl.when(slot == group - 1)
        def _():
            first = pl.multiple_of(at - (group - 1), group)

            def turn(j, carry):
                for c in range(0, width, LANES):
                    cols = pl.ds(c, LANES)
                    rows = pl.ds(pl.multiple_of(j * chunk, chunk), chunk)
                    piece = mid_group[:, rows, cols].astype(F32)
                    piece = jnp.swapaxes(piece, 0, 1).astype(BF16)
                    mid_send[pl.ds(j * tall, tall), :, pl.ds(first, group), cols] = (
                        piece.reshape(tall, inner, group, LANES)
                    )
                return carry

            lax.fori_loop(0, inner_size // chunk, turn, 0)

    @pl.when(step == third - 1)
    def _():
        mb_all.wait_send()
        for s in order:
            to = lax.rem(me + s, n)
            pltpu.make_async_remote_copy(
                src_ref=mid_send.at[to], dst_ref=mid_recv.at[me],
                send_sem=mid_out, recv_sem=mid_in,
                device_id=(part, to), device_id_type=MESH,
            ).start()
        mid_local.start()
        mb_all.wait_recv()
        mb_local.wait()

        def turn(j, carry):
            for c in range(0, width, LANES):
                cols = pl.ds(c, LANES)
                piece = mb_recv[pl.ds(j * tall, tall), :, :, cols]
                piece = piece.reshape(chunk, outer, LANES).astype(F32)
                piece = jnp.swapaxes(piece, 0, 1).astype(BF16)
                rows = pl.ds(pl.multiple_of(j * chunk, chunk), chunk)
                mb_here[:, rows, cols] = piece
            return carry

        lax.fori_loop(0, inner_size // chunk, turn, 0)
        gl_ref[...] = jnp.zeros_like(gl_ref)

    @pl.when(step >= third)
    def _():
        tok, tok_f, gate, mixed = gated()
        back = mb_here[step - third]
        fg_ref[0] = dot(back, mixed, 1, 1).astype(BF16)
        mixed_back = dot(ff_ref[0], back, 0, 0)
        slope = (mixed_back * tok_f * gate * (1.0 - gate)).astype(BF16)
        tg_ref[0] = (mixed_back * gate + dot(slope, w_ref[...], 1, 1)).astype(BF16)
        gl_ref[...] += dot(tok, slope, 0, 0)

    @pl.when(step == last)
    def _():
        mid_all.wait_send()
        mid_all.wait_recv()
        mid_local.wait()


def second_kernel(cot_ref, mid_ref, sg_ref):
    n, _, outer, width = mid_ref.shape
    middle = mid_ref[:, 0]
    if outer % 16:
        middle = middle.astype(F32).reshape(n * outer, width).astype(BF16)
    else:
        middle = middle.reshape(n * outer, width)
    sg_ref[0] = dot(cot_ref[0], middle, 1, 1).astype(BF16)


def on_device(n, tokens, cotangent, first_factor, second_factor, gate_weight):
    width = tokens.shape[1]
    outer, inner_size = first_factor.shape[:2]
    inner, outer_size = second_factor.shape[:2]
    tok3 = tokens.reshape(outer, inner_size, width)
    back = cotangent.reshape(inner, outer_size, width)
    group = min(16, outer)
    steps = inner + 2 * outer

    def by_inner(i):
        return (jnp.minimum(i, inner - 1), 0, 0)

    def by_outer(i):
        return (lax.rem(jnp.maximum(i - inner, 0), outer), 0, 0)

    def by_back(i):
        return (jnp.maximum(i - inner - outer, 0), 0, 0)

    def whole(i):
        return (0, 0)

    moved = (n, inner, outer, width)
    token_grad, first_grad, gate_local, middle_here = pl.pallas_call(
        functools.partial(exchange_kernel, n, outer, inner, group),
        grid=(steps,),
        out_shape=(
            jax.ShapeDtypeStruct(tok3.shape, BF16),
            jax.ShapeDtypeStruct(first_factor.shape, BF16),
            jax.ShapeDtypeStruct(gate_weight.shape, F32),
            jax.ShapeDtypeStruct(moved, BF16),
        ),
        in_specs=[
            pl.BlockSpec((1, inner_size, width), by_outer),
            pl.BlockSpec((1, outer_size, width), by_inner),
            pl.BlockSpec((1, inner_size, inner_size), by_outer),
            pl.BlockSpec((1, outer_size, outer_size), by_inner),
            pl.BlockSpec(gate_weight.shape, whole),
        ],
        out_specs=(
            pl.BlockSpec((1, inner_size, width), by_back),
            pl.BlockSpec((1, inner_size, inner_size), by_back),
            pl.BlockSpec(gate_weight.shape, whole),
            pl.BlockSpec(memory_space=pl.ANY),
        ),
        scratch_shapes=[
            pltpu.VMEM(moved, BF16),
            pltpu.VMEM(moved, BF16),
            pltpu.VMEM((outer, inner_size, width), BF16),
            pltpu.VMEM((group, inner_size, width), BF16),
            pltpu.VMEM(moved, BF16),
        ] + [pltpu.SemaphoreType.DMA] * 6,
        compiler_params=pltpu.CompilerParams(
            collective_id=0, has_side_effects=True, vmem_limit_bytes=56 * 2**20
        ),
        name="exchange",
    )(tok3, back, first_factor, second_factor, gate_weight)
    gate_grad = lax.psum(gate_local, "seq")
    second_grad = pl.pallas_call(
        second_kernel,
        grid=(inner,),
        out_shape=jax.ShapeDtypeStruct(second_factor.shape, BF16),
        in_specs=[
            pl.BlockSpec((1, outer_size, width), lambda i: (i, 0, 0)),
            pl.BlockSpec((n, 1, outer, width), lambda i: (0, i, 0, 0)),
        ],
        out_specs=pl.BlockSpec((1, outer_size, outer_size), lambda i: (i, 0, 0)),
        compiler_params=pltpu.CompilerParams(vmem_limit_bytes=32 * 2**20),
        name="second",
    )(back, middle_here)
    return (
        token_grad.reshape(tokens.shape),
        first_grad,
        second_grad,
        gate_grad.astype(BF16),
    )


def solution(mesh):
    return jax.shard_map(
        functools.partial(on_device, mesh.shape["seq"]),
        mesh=mesh,
        in_specs=(
            P(("parts", "seq"), None),
            P(("parts", "seq"), None),
            P("seq", None, None),
            P("seq", None, None),
            P(),
        ),
        out_specs=(
            P(("parts", "seq"), None),
            P(("parts", "seq"), None, None),
            P(("parts", "seq"), None, None),
            P("parts", None),
        ),
        check_vma=False,
    )
```

```python
import functools

import jax
import jax.numpy as jnp
from jax import lax
from jax.experimental import pallas as pl
from jax.experimental.pallas import tpu as pltpu
from jax.sharding import PartitionSpec as P

MESH = pl.DeviceIdType.MESH
F32 = jnp.float32
BF16 = jnp.bfloat16
LANES = 128


def dot(x, y, x_dim, y_dim):
    return lax.dot_general(
        x, y, (((x_dim,), (y_dim,)), ((), ())), preferred_element_type=F32
    )


def send_order(n):
    quarters = [list(range(q * n // 4, (q + 1) * n // 4)) for q in (2, 1, 3, 0)]
    order = [s for group in zip(*quarters) for s in group]
    return [s for s in order if s != 0]


def exchange_kernel(
    n, outer, inner, group,
    tok_ref, cot_ref, ff_ref, sf_ref, w_ref,
    tg_ref, fg_ref, gg_ref, mid_recv,
    mb_send, mb_recv, mb_here, mid_group, mid_send,
    gl_ref, slabs, own_slab, far_slab, gg_parts,
    mb_out, mb_in, mb_own, mid_out, mid_in, mid_own,
    slab_out, slab_in, far_out, far_in, gg_out, gg_in,
):
    part, me = lax.axis_index("parts"), lax.axis_index("seq")
    step = pl.program_id(0)
    width = tok_ref.shape[2]
    inner_size = tok_ref.shape[1]
    batch = min(4, inner)
    batches = inner // batch
    second, third = inner, inner + outer
    last = inner + 2 * outer - 1
    order = send_order(n)

    def remote(src, dst, out_sem, in_sem, to):
        return pltpu.make_async_remote_copy(
            src_ref=src, dst_ref=dst, send_sem=out_sem, recv_sem=in_sem,
            device_id=(part, to), device_id_type=MESH,
        )

    def mb_batch(k):
        some = (pl.ds(0, n - 1), pl.ds(0, batch))
        return remote(
            mb_send.at[some], mb_recv.at[some], mb_out.at[k], mb_in.at[k], lax.rem(me + 1, n)
        )

    others = pl.ds(0, n - 1)
    mid_all = remote(
        mid_send.at[others], mid_recv.at[others], mid_out, mid_in, lax.rem(me + 1, n)
    )
    mb_local = pltpu.make_async_copy(mb_send.at[me], mb_recv.at[me], mb_own)
    mid_local = pltpu.make_async_copy(mid_send.at[me], mid_recv.at[me], mid_own)

    @pl.when(step == 0)
    def _():
        barrier = pltpu.get_barrier_semaphore()
        for s in range(1, n):
            pl.semaphore_signal(
                barrier, inc=1, device_id=(part, lax.rem(me + s, n)), device_id_type=MESH
            )
        pl.semaphore_wait(barrier, n - 1)

    @pl.when(step < second)
    def _():
        made = dot(sf_ref[0], cot_ref[0], 0, 0)
        mb_send[:, step] = made.reshape(n, outer, width).astype(BF16)

        @pl.when(lax.rem(step, batch) == batch - 1)
        def _():
            k = step // batch
            rows = pl.ds(step - (batch - 1), batch)
            for s in order:
                to = lax.rem(me + s, n)
                remote(
                    mb_send.at[to, rows], mb_recv.at[me, rows], mb_out.at[k], mb_in.at[k], to
                ).start()

    @pl.when(step == second)
    def _():
        mb_local.start()

    def gated():
        tok = tok_ref[0]
        tok_f = tok.astype(F32)
        gate = jax.nn.sigmoid(dot(tok, w_ref[...], 1, 0))
        return tok, tok_f, gate, (tok_f * gate).astype(BF16)

    tall = 16 // inner if inner < 16 else 1
    chunk = tall * inner

    @pl.when((step >= second) & (step < third))
    def _():
        at = step - second
        _, _, _, mixed = gated()
        slot = lax.rem(at, group)
        mid_group[slot] = dot(ff_ref[0], mixed, 1, 0).astype(BF16)

        @pl.when(slot == group - 1)
        def _():
            first = pl.multiple_of(at - (group - 1), group)

            def turn(j, carry):
                for c in range(0, width, LANES):
                    cols = pl.ds(c, LANES)
                    rows = pl.ds(pl.multiple_of(j * chunk, chunk), chunk)
                    piece = mid_group[:, rows, cols].astype(F32)
                    piece = jnp.swapaxes(piece, 0, 1).astype(BF16)
                    mid_send[pl.ds(j * tall, tall), :, pl.ds(first, group), cols] = (
                        piece.reshape(tall, inner, group, LANES)
                    )
                return carry

            lax.fori_loop(0, inner_size // chunk, turn, 0)

    @pl.when(step == third - 1)
    def _():
        for k in range(batches - 1):
            mb_batch(k).wait_send()
        for s in order:
            to = lax.rem(me + s, n)
            remote(mid_send.at[to], mid_recv.at[me], mid_out, mid_in, to).start()
        mid_local.start()
        mb_batch(batches - 1).wait_send()
        for k in range(batches):
            mb_batch(k).wait_recv()
        mb_local.wait()

        def turn(j, carry):
            for c in range(0, width, LANES):
                cols = pl.ds(c, LANES)
                piece = mb_recv[pl.ds(j * tall, tall), :, :, cols]
                piece = piece.reshape(chunk, outer, LANES).astype(F32)
                piece = jnp.swapaxes(piece, 0, 1).astype(BF16)
                rows = pl.ds(pl.multiple_of(j * chunk, chunk), chunk)
                mb_here[:, rows, cols] = piece
            return carry

        lax.fori_loop(0, inner_size // chunk, turn, 0)
        gl_ref[...] = jnp.zeros_like(gl_ref)

    @pl.when(step >= third)
    def _():
        tok, tok_f, gate, mixed = gated()
        back = mb_here[step - third]
        fg_ref[0] = dot(back, mixed, 1, 1).astype(BF16)
        mixed_back = dot(ff_ref[0], back, 0, 0)
        slope = (mixed_back * tok_f * gate * (1.0 - gate)).astype(BF16)
        tg_ref[0] = (mixed_back * gate + dot(slope, w_ref[...], 1, 1)).astype(BF16)
        gl_ref[...] += dot(tok, slope, 0, 0)

    @pl.when(step == last)
    def _():
        half = n // 2
        mine, base = lax.rem(me, half), (me // half) * half
        far = lax.rem(me + half, n)
        tall_slab = width // half

        def slab(i):
            return gl_ref.at[pl.ds(pl.multiple_of(i * tall_slab, tall_slab), tall_slab)]

        for s in range(1, half):
            to = lax.rem(mine + s, half)
            remote(slab(to), slabs.at[mine], slab_out, slab_in, base + to).start()
        some = pl.ds(0, half - 1)
        flat = pl.ds(0, (half - 1) * tall_slab)
        sent = remote(gl_ref.at[flat], gl_ref.at[flat], slab_out, slab_in, far)
        sent.wait_send()
        remote(slabs.at[some], slabs.at[some], slab_out, slab_in, far).wait_recv()
        total = slab(mine)[...]
        for s in range(1, half):
            total = total + slabs[lax.rem(mine + s, half)]
        own_slab[...] = total
        across = remote(own_slab, far_slab, far_out, far_in, far)
        across.start()
        across.wait()
        gg_parts[mine] = (own_slab[...] + far_slab[...]).astype(BF16)
        for s in range(1, half):
            to = lax.rem(mine + s, half)
            remote(gg_parts.at[mine], gg_parts.at[mine], gg_out, gg_in, base + to).start()
        shared = remote(gg_parts.at[some], gg_parts.at[some], gg_out, gg_in, far)
        shared.wait_send()
        shared.wait_recv()
        gg_ref[...] = gg_parts[...].reshape(width, width)
        mid_all.wait_send()
        mid_all.wait_recv()
        mid_local.wait()


def second_kernel(cot_ref, mid_ref, tg_ref, fg_ref, gg_ref, sg_ref, tg_out, fg_out, gg_out):
    tg_out[...] = tg_ref[...]
    fg_out[...] = fg_ref[...]
    gg_out[...] = gg_ref[...]
    n, _, outer, width = mid_ref.shape
    middle = mid_ref[:, 0]
    if outer % 16:
        middle = middle.astype(F32).reshape(n * outer, width).astype(BF16)
    else:
        middle = middle.reshape(n * outer, width)
    sg_ref[0] = dot(cot_ref[0], middle, 1, 1).astype(BF16)


def on_device(n, tokens, cotangent, first_factor, second_factor, gate_weight):
    width = tokens.shape[1]
    outer, inner_size = first_factor.shape[:2]
    inner, outer_size = second_factor.shape[:2]
    tok3 = tokens.reshape(outer, inner_size, width)
    back = cotangent.reshape(inner, outer_size, width)
    group = min(16, outer)
    half = n // 2
    batches = inner // min(4, inner)
    steps = inner + 2 * outer

    def by_inner(i):
        return (jnp.minimum(i, inner - 1), 0, 0)

    def by_outer(i):
        return (lax.rem(jnp.maximum(i - inner, 0), outer), 0, 0)

    def by_back(i):
        return (jnp.maximum(i - inner - outer, 0), 0, 0)

    def whole(i):
        return (0, 0)

    moved = (n, inner, outer, width)
    token_grad, first_grad, gate_grad, middle_here = pl.pallas_call(
        functools.partial(exchange_kernel, n, outer, inner, group),
        grid=(steps,),
        out_shape=(
            jax.ShapeDtypeStruct(tok3.shape, BF16),
            jax.ShapeDtypeStruct(first_factor.shape, BF16),
            jax.ShapeDtypeStruct(gate_weight.shape, BF16),
            jax.ShapeDtypeStruct(moved, BF16),
        ),
        in_specs=[
            pl.BlockSpec((1, inner_size, width), by_outer),
            pl.BlockSpec((1, outer_size, width), by_inner),
            pl.BlockSpec((1, inner_size, inner_size), by_outer),
            pl.BlockSpec((1, outer_size, outer_size), by_inner),
            pl.BlockSpec(gate_weight.shape, whole),
        ],
        out_specs=(
            pl.BlockSpec((1, inner_size, width), by_back),
            pl.BlockSpec((1, inner_size, inner_size), by_back),
            pl.BlockSpec(gate_weight.shape, whole),
            pl.BlockSpec(memory_space=pl.ANY),
        ),
        scratch_shapes=[
            pltpu.VMEM(moved, BF16),
            pltpu.VMEM(moved, BF16),
            pltpu.VMEM((outer, inner_size, width), BF16),
            pltpu.VMEM((group, inner_size, width), BF16),
            pltpu.VMEM(moved, BF16),
            pltpu.VMEM((width, width), F32),
            pltpu.VMEM((half, width // half, width), F32),
            pltpu.VMEM((width // half, width), F32),
            pltpu.VMEM((width // half, width), F32),
            pltpu.VMEM((half, width // half, width), BF16),
        ] + [pltpu.SemaphoreType.DMA((batches,))] * 2 + [pltpu.SemaphoreType.DMA] * 10,
        compiler_params=pltpu.CompilerParams(
            collective_id=0, has_side_effects=True, vmem_limit_bytes=56 * 2**20
        ),
        name="exchange",
    )(tok3, back, first_factor, second_factor, gate_weight)
    per = outer // inner
    tokens_spec = pl.BlockSpec((per, inner_size, width), lambda i: (i, 0, 0))
    first_spec = pl.BlockSpec((per, inner_size, inner_size), lambda i: (i, 0, 0))
    gate_spec = pl.BlockSpec(gate_weight.shape, whole)
    second_grad, token_grad, first_grad, gate_grad = pl.pallas_call(
        second_kernel,
        grid=(inner,),
        out_shape=(
            jax.ShapeDtypeStruct(second_factor.shape, BF16),
            jax.ShapeDtypeStruct(tok3.shape, BF16),
            jax.ShapeDtypeStruct(first_factor.shape, BF16),
            jax.ShapeDtypeStruct(gate_weight.shape, BF16),
        ),
        in_specs=[
            pl.BlockSpec((1, outer_size, width), lambda i: (i, 0, 0)),
            pl.BlockSpec((n, 1, outer, width), lambda i: (0, i, 0, 0)),
            tokens_spec,
            first_spec,
            gate_spec,
        ],
        out_specs=(
            pl.BlockSpec((1, outer_size, outer_size), lambda i: (i, 0, 0)),
            tokens_spec,
            first_spec,
            gate_spec,
        ),
        compiler_params=pltpu.CompilerParams(vmem_limit_bytes=60 * 2**20),
        name="second",
    )(back, middle_here, token_grad, first_grad, gate_grad)
    return token_grad.reshape(tokens.shape), first_grad, second_grad, gate_grad


def solution(mesh):
    return jax.shard_map(
        functools.partial(on_device, mesh.shape["seq"]),
        mesh=mesh,
        in_specs=(
            P(("parts", "seq"), None),
            P(("parts", "seq"), None),
            P("seq", None, None),
            P("seq", None, None),
            P(),
        ),
        out_specs=(
            P(("parts", "seq"), None),
            P(("parts", "seq"), None, None),
            P(("parts", "seq"), None, None),
            P("parts", None),
        ),
        check_vma=False,
    )
```

```python
import functools

import jax
import jax.numpy as jnp
from jax import lax
from jax.experimental import pallas as pl
from jax.experimental.pallas import tpu as pltpu
from jax.sharding import PartitionSpec as P

MESH = pl.DeviceIdType.MESH
F32 = jnp.float32
BF16 = jnp.bfloat16
LANES = 128


def dot(x, y, x_dim, y_dim):
    return lax.dot_general(
        x, y, (((x_dim,), (y_dim,)), ((), ())), preferred_element_type=F32
    )


def send_order(n):
    quarters = [list(range(q * n // 4, (q + 1) * n // 4)) for q in (2, 1, 3, 0)]
    order = [s for group in zip(*quarters) for s in group]
    return [s for s in order if s != 0]


def exchange_kernel(
    n, outer, inner, group,
    tok_ref, cot_ref, ff_ref, sf_ref, w_ref,
    tg_ref, fg_ref, gg_ref, mid_recv,
    flat, spare, mb_recv, mid_group, mid_send,
    gl_ref, slabs, own_slab, far_slab, gg_parts,
    mb_out, mb_in, mb_own, mid_out, mid_in, mid_own,
    slab_out, slab_in, far_out, far_in, gg_out, gg_in,
):
    part, me = lax.axis_index("parts"), lax.axis_index("seq")
    step = pl.program_id(0)
    width = tok_ref.shape[2]
    inner_size = tok_ref.shape[1]
    batch = min(4, inner)
    batches = inner // batch
    second, third = inner, inner + outer
    last = inner + 2 * outer - 1
    order = send_order(n)

    def remote(src, dst, out_sem, in_sem, to):
        return pltpu.make_async_remote_copy(
            src_ref=src, dst_ref=dst, send_sem=out_sem, recv_sem=in_sem,
            device_id=(part, to), device_id_type=MESH,
        )

    def mb_batch(k):
        some = mb_recv.at[pl.ds(0, n - 1), pl.ds(0, batch)]
        return remote(some, some, mb_out.at[k], mb_in.at[k], lax.rem(me + 1, n))

    others = pl.ds(0, n - 1)
    mid_all = remote(
        mid_send.at[others], mid_recv.at[others], mid_out, mid_in, lax.rem(me + 1, n)
    )
    mb_send = spare if outer % 16 else flat.reshape(n, inner, outer, width)
    mb_here = flat.reshape(outer, inner_size, width)
    mb_local = pltpu.make_async_copy(mb_send.at[me], mb_recv.at[me], mb_own)
    mid_local = pltpu.make_async_copy(mid_send.at[me], mid_recv.at[me], mid_own)

    def send_middle(start, stop, rows):
        for s in order[start:stop]:
            to = lax.rem(me + s, n)
            remote(
                mid_send.at[to, :, rows], mid_recv.at[me, :, rows], mid_out, mid_in, to
            ).start()

    first_rows = pl.ds(0, group)
    other_rows = pl.ds(group, outer - group)
    marks = [(n - 1) * k // 4 for k in (0, 2, 3, 4)]

    @pl.when(step == 0)
    def _():
        barrier = pltpu.get_barrier_semaphore()
        for s in range(1, n):
            pl.semaphore_signal(
                barrier, inc=1, device_id=(part, lax.rem(me + s, n)), device_id_type=MESH
            )
        pl.semaphore_wait(barrier, n - 1)

    @pl.when(step < second)
    def _():
        made = dot(sf_ref[0], cot_ref[0], 0, 0)
        mb_send[:, step] = made.reshape(n, outer, width).astype(BF16)

        @pl.when(lax.rem(step, batch) == batch - 1)
        def _():
            k = step // batch
            rows = pl.ds(step - (batch - 1), batch)
            for s in order:
                to = lax.rem(me + s, n)
                remote(
                    mb_send.at[to, rows], mb_recv.at[me, rows], mb_out.at[k], mb_in.at[k], to
                ).start()

    @pl.when(step == second)
    def _():
        mb_local.start()

    def gated():
        tok = tok_ref[0]
        tok_f = tok.astype(F32)
        gate = jax.nn.sigmoid(dot(tok, w_ref[...], 1, 0))
        return tok, tok_f, gate, (tok_f * gate).astype(BF16)

    tall = 16 // inner if inner < 16 else 1
    chunk = tall * inner

    @pl.when((step >= second) & (step < third))
    def _():
        at = step - second
        _, _, _, mixed = gated()
        slot = lax.rem(at, group)
        mid_group[slot] = dot(ff_ref[0], mixed, 1, 0).astype(BF16)

        @pl.when(slot == group - 1)
        def _():
            first = pl.multiple_of(at - (group - 1), group)

            def turn(j, carry):
                for c in range(0, width, LANES):
                    cols = pl.ds(c, LANES)
                    rows = pl.ds(pl.multiple_of(j * chunk, chunk), chunk)
                    piece = mid_group[:, rows, cols].astype(F32)
                    piece = jnp.swapaxes(piece, 0, 1).astype(BF16)
                    mid_send[pl.ds(j * tall, tall), :, pl.ds(first, group), cols] = (
                        piece.reshape(tall, inner, group, LANES)
                    )
                return carry

            lax.fori_loop(0, inner_size // chunk, turn, 0)

    @pl.when(step == third - 1)
    def _():
        for k in range(batches - 1):
            mb_batch(k).wait_send()
        send_middle(0, n - 1, first_rows)
        mid_local.start()
        mb_batch(batches - 1).wait_send()
        for k in range(batches):
            mb_batch(k).wait_recv()
        mb_local.wait()

        def turn(j, carry):
            for c in range(0, width, LANES):
                cols = pl.ds(c, LANES)
                piece = mb_recv[pl.ds(j * tall, tall), :, :, cols]
                piece = piece.reshape(chunk, outer, LANES).astype(F32)
                piece = jnp.swapaxes(piece, 0, 1).astype(BF16)
                rows = pl.ds(pl.multiple_of(j * chunk, chunk), chunk)
                mb_here[:, rows, cols] = piece
            return carry

        lax.fori_loop(0, inner_size // chunk, turn, 0)
        gl_ref[...] = jnp.zeros_like(gl_ref)

    @pl.when(step >= third)
    def _():
        tok, tok_f, gate, mixed = gated()
        at = step - third
        back = mb_here[at]
        fg_ref[at] = dot(back, mixed, 1, 1).astype(BF16)
        mixed_back = dot(ff_ref[0], back, 0, 0)
        slope = (mixed_back * tok_f * gate * (1.0 - gate)).astype(BF16)
        tg_ref[at] = (mixed_back * gate + dot(slope, w_ref[...], 1, 1)).astype(BF16)
        gl_ref[...] += dot(tok, slope, 0, 0)

    if outer > group:
        @pl.when(step == third + outer // 2)
        def _():
            send_middle(marks[0], marks[1], other_rows)

    @pl.when(step == last)
    def _():
        half = n // 2
        mine, base = lax.rem(me, half), (me // half) * half
        far = lax.rem(me + half, n)
        tall_slab = width // half

        def slab(i):
            return gl_ref.at[pl.ds(pl.multiple_of(i * tall_slab, tall_slab), tall_slab)]

        for s in range(1, half):
            to = lax.rem(mine + s, half)
            remote(slab(to), slabs.at[mine], slab_out, slab_in, base + to).start()
        if outer > group:
            send_middle(marks[1], marks[2], other_rows)
        some = pl.ds(0, half - 1)
        rows = pl.ds(0, (half - 1) * tall_slab)
        sent = remote(gl_ref.at[rows], gl_ref.at[rows], slab_out, slab_in, far)
        sent.wait_send()
        remote(slabs.at[some], slabs.at[some], slab_out, slab_in, far).wait_recv()
        total = slab(mine)[...]
        for s in range(1, half):
            total = total + slabs[lax.rem(mine + s, half)]
        own_slab[...] = total
        across = remote(own_slab, far_slab, far_out, far_in, far)
        across.start()
        if outer > group:
            send_middle(marks[2], marks[3], other_rows)
        across.wait()
        gg_parts[mine] = (own_slab[...] + far_slab[...]).astype(BF16)
        for s in range(1, half):
            to = lax.rem(mine + s, half)
            remote(gg_parts.at[mine], gg_parts.at[mine], gg_out, gg_in, base + to).start()
        shared = remote(gg_parts.at[some], gg_parts.at[some], gg_out, gg_in, far)
        shared.wait_send()
        shared.wait_recv()
        gg_ref[...] = gg_parts[...].reshape(width, width)
        mid_all.wait_send()
        mid_all.wait_recv()
        mid_local.wait()


def second_kernel(
    cot_ref, mid_ref, tg_ref, fg_ref, sg_ref, tg_out, fg_out, back, cot_sems, sems
):
    step, steps = pl.program_id(0), pl.num_programs(0)
    n, _, outer, width = mid_ref.shape
    copies = [
        pltpu.make_async_copy(tg_ref, tg_out, sems.at[0]),
        pltpu.make_async_copy(fg_ref, fg_out, sems.at[1]),
    ]
    slot = lax.rem(step, 2)

    def fetch(block, to):
        return pltpu.make_async_copy(cot_ref.at[block], back.at[to], cot_sems.at[to])

    @pl.when(step == 0)
    def _():
        fetch(0, 0).start()
        for copy in copies:
            copy.start()

    @pl.when(step + 1 < steps)
    def _():
        fetch(step + 1, 1 - slot).start()

    fetch(step, slot).wait()
    middle = mid_ref[:, 0]
    if outer % 16:
        middle = middle.astype(F32).reshape(n * outer, width).astype(BF16)
    else:
        middle = middle.reshape(n * outer, width)
    sg_ref[0] = dot(back[slot], middle, 1, 1).astype(BF16)

    @pl.when(step == steps - 1)
    def _():
        for copy in copies:
            copy.wait()


def on_device(n, tokens, cotangent, first_factor, second_factor, gate_weight):
    width = tokens.shape[1]
    outer, inner_size = first_factor.shape[:2]
    inner, outer_size = second_factor.shape[:2]
    tok3 = tokens.reshape(outer, inner_size, width)
    back = cotangent.reshape(inner, outer_size, width)
    group = min(16, outer)
    half = n // 2
    batches = inner // min(4, inner)
    steps = inner + 2 * outer

    def by_inner(i):
        return (jnp.minimum(i, inner - 1), 0, 0)

    def by_outer(i):
        return (lax.rem(jnp.maximum(i - inner, 0), outer), 0, 0)

    def whole(i):
        return (0, 0)

    kept = pl.BlockSpec(memory_space=pltpu.VMEM)
    moved = (n, inner, outer, width)
    token_grad, first_grad, gate_grad, middle_here = pl.pallas_call(
        functools.partial(exchange_kernel, n, outer, inner, group),
        grid=(steps,),
        out_shape=(
            pltpu.VMEM(tok3.shape, BF16),
            pltpu.VMEM(first_factor.shape, BF16),
            jax.ShapeDtypeStruct(gate_weight.shape, BF16),
            jax.ShapeDtypeStruct(moved, BF16),
        ),
        in_specs=[
            pl.BlockSpec((1, inner_size, width), by_outer),
            pl.BlockSpec((1, outer_size, width), by_inner),
            pl.BlockSpec((1, inner_size, inner_size), by_outer),
            pl.BlockSpec((1, outer_size, outer_size), by_inner),
            pl.BlockSpec(gate_weight.shape, whole),
        ],
        out_specs=(
            kept,
            kept,
            pl.BlockSpec(gate_weight.shape, whole),
            pl.BlockSpec(memory_space=pl.ANY),
        ),
        scratch_shapes=[
            pltpu.VMEM((outer * inner_size, width), BF16),
            pltpu.VMEM(moved if outer % 16 else (16, LANES), BF16),
            pltpu.VMEM(moved, BF16),
            pltpu.VMEM((group, inner_size, width), BF16),
            pltpu.VMEM(moved, BF16),
            pltpu.VMEM((width, width), F32),
            pltpu.VMEM((half, width // half, width), F32),
            pltpu.VMEM((width // half, width), F32),
            pltpu.VMEM((width // half, width), F32),
            pltpu.VMEM((half, width // half, width), BF16),
        ] + [pltpu.SemaphoreType.DMA((batches,))] * 2 + [pltpu.SemaphoreType.DMA] * 10,
        compiler_params=pltpu.CompilerParams(
            collective_id=0, has_side_effects=True, vmem_limit_bytes=40 * 2**20
        ),
        name="exchange",
    )(tok3, back, first_factor, second_factor, gate_weight)
    second_grad, token_grad, first_grad = pl.pallas_call(
        second_kernel,
        grid=(inner,),
        out_shape=(
            jax.ShapeDtypeStruct(second_factor.shape, BF16),
            jax.ShapeDtypeStruct(tok3.shape, BF16),
            jax.ShapeDtypeStruct(first_factor.shape, BF16),
        ),
        in_specs=[
            pl.BlockSpec(memory_space=pltpu.HBM),
            pl.BlockSpec((n, 1, outer, width), lambda i: (0, i, 0, 0)),
            kept,
            kept,
        ],
        out_specs=(
            pl.BlockSpec((1, outer_size, outer_size), lambda i: (i, 0, 0)),
            pl.BlockSpec(memory_space=pl.ANY),
            pl.BlockSpec(memory_space=pl.ANY),
        ),
        scratch_shapes=[
            pltpu.VMEM((2, outer_size, width), BF16),
            pltpu.SemaphoreType.DMA((2,)),
            pltpu.SemaphoreType.DMA((2,)),
        ],
        compiler_params=pltpu.CompilerParams(vmem_limit_bytes=8 * 2**20),
        name="second",
    )(back, middle_here, token_grad, first_grad)
    return token_grad.reshape(tokens.shape), first_grad, second_grad, gate_grad


def solution(mesh):
    return jax.shard_map(
        functools.partial(on_device, mesh.shape["seq"]),
        mesh=mesh,
        in_specs=(
            P(("parts", "seq"), None),
            P(("parts", "seq"), None),
            P("seq", None, None),
            P("seq", None, None),
            P(),
        ),
        out_specs=(
            P(("parts", "seq"), None),
            P(("parts", "seq"), None, None),
            P(("parts", "seq"), None, None),
            P("parts", None),
        ),
        check_vma=False,
    )
```
